32 devices in a mesh: grid: 2 (over x), rank: 4 (over y, core), term: 4 (over z).
Axes of the slice: x: 2, y: 2, z: 4, core: 2. Of those that a mesh axis runs over, the one named last changes fastest.
Arguments:
- rhs: float32 [128, 4, 256], P('rank', 'grid')
- coef: float32 [12, 4, 256], P('term', 'grid'), may hold values from 0.03 to 0.3
- env: float32 [12, 128, 128], P('term', 'rank'), as said below
Outputs:
- solution: float32 [128, 4, 256], P('rank', 'grid')
- residual: float32 [128, 4, 256], P('rank', 'grid')
The draws below stay inside these ranges and needn't reach their ends.
Inputs may be any that keep to these rules, and one draw needn't show every extreme that they name: env[k] is a symmetric matrix for every k.
All inputs are finite; a program needn't handle non-finite values.
Results may differ from the reference program's by a relative error of at most 0.0003.
Values sent between devices are 32-bit elements; how exact they have to be, the bound alone decides.
A program may use at most 64 MiB of HBM per device.

```python
import math
import jax
import jax.numpy as jnp
from jax import lax

K = 12
R = 128
NY = 256
ITERS = 4
NX = 4


def draw_rhs(key, part):
    subkeys = jax.random.split(key, 3)
    rank_scale = jnp.exp(jax.random.uniform(subkeys[1], (R, 1, 1), jnp.float32, 0.0, math.log(10.0)))
    x_centre = (jnp.arange(NX, dtype=jnp.float32) + 0.5) / NX
    row_scale = jnp.exp(jax.random.uniform(subkeys[2], (1, NX, 1), jnp.float32, 0.0, math.log(10.0)))
    row_scale = row_scale * (1.0 + 2.0 * x_centre)[None, :, None] / 3.0
    noise = jnp.clip(jax.random.normal(subkeys[0], (R, NX, NY), jnp.float32), -4.0, 4.0)
    return 0.3 * noise * rank_scale * row_scale


def draw_env(key, part):
    subkeys = jax.random.split(jax.random.fold_in(key, 7), 2)
    scatter_part = jax.random.uniform(subkeys[0], (K, R, R), jnp.float32, -1.0 / R, 1.0 / R)
    upper_part = jnp.triu(scatter_part, 1)
    symmetric = upper_part + jnp.swapaxes(upper_part, 1, 2)
    diag_part = 1.0 + jax.random.uniform(subkeys[1], (K, R), jnp.float32, 0.0, 1.0)
    return symmetric + diag_part[:, :, None] * jnp.eye(R, dtype=jnp.float32)[None]


def levels(own_key, dims, cuts, low, high):
    def one(dim, shards_of):
        draws = jax.random.uniform(jax.random.fold_in(jax.random.fold_in(own_key, 6), dim), (shards_of,), jnp.float32, low / len(cuts), high / len(cuts))
        return jnp.repeat(jnp.exp(draws), dims[dim] // shards_of).reshape((-1,) + (1,) * (len(dims) - dim - 1))

    loudness = one(*cuts[0])
    for cut in cuts[1:]:
        loudness = loudness * one(*cut)
    return loudness


def setup_inputs(seed: int = 0) -> dict:
    splits = jax.random.split(jax.random.key(seed), 4)
    rhs = draw_rhs(jax.random.fold_in(splits[3], 71), 0)
    coef = jnp.clip(jnp.exp(math.log(0.3) - 2.3025852 * jax.random.uniform(splits[1], (K, NX, NY), jnp.float32) ** levels(splits[1], (K, NX, NY), ((0, 4), (1, 2)), -0.2, 0.2)), 0.03, 0.3)
    env = draw_env(jax.random.fold_in(splits[3], 71), 0)
    return dict(rhs=rhs, coef=coef, env=env)


def face_weights(padded):
    wide = jnp.pad(padded, ((0, 0), (0, 0), (1, 1)))
    centre = wide[:, 1:-1, 1:-1]
    face_up = 0.5 * (centre + wide[:, 2:, 1:-1])
    face_down = 0.5 * (centre + wide[:, :-2, 1:-1])
    face_right = 0.5 * (centre + wide[:, 1:-1, 2:])
    face_left = 0.5 * (centre + wide[:, 1:-1, :-2])
    return (face_up + face_down + face_right + face_left, face_up, face_down, face_right, face_left)


def apply_faces(field, faces):
    middle = field[..., 1:-1, :]
    sideways = jnp.pad(middle, [(0, 0)] * (middle.ndim - 1) + [(1, 1)])
    total, face_up, face_down, face_right, face_left = faces
    return (total * middle - face_up * field[..., 2:, :] - face_down * field[..., :-2, :]
            - face_right * sideways[..., 2:] - face_left * sideways[..., :-2])


def reference(rhs, coef, env):
    faces = face_weights(jnp.pad(coef, ((0, 0), (1, 1), (0, 0))))

    def operate(field):
        padded = jnp.pad(field, ((0, 0), (1, 1), (0, 0)))
        result = jnp.zeros(field.shape, jnp.float32)
        for term_index in range(K):
            term_faces = tuple(weights[term_index] for weights in faces)
            stenciled = apply_faces(padded, term_faces)
            result = result + jnp.einsum("rs,rxy->sxy", env[term_index], stenciled,
                                         precision=lax.Precision.HIGHEST)
        return result

    solution = jnp.zeros(rhs.shape, jnp.float32)
    residual = rhs
    direction = rhs
    norm_now = jnp.sum(residual * residual)
    for step in range(ITERS):
        image = operate(direction)
        alpha = norm_now / jnp.sum(direction * image)
        solution = solution + alpha * direction
        residual = residual - alpha * image
        norm_next = jnp.sum(residual * residual)
        direction = residual + (norm_next / norm_now) * direction
        norm_now = norm_next
    return solution, residual
```

```python
import functools

import jax
import jax.numpy as jnp
from jax import lax
from jax.experimental import pallas as pl
from jax.experimental.pallas import tpu as pltpu
from jax.sharding import PartitionSpec as P

ITERS = 4
MESH = pl.DeviceIdType.MESH


def padded_2(block, sides, width):
    for axis, dim in sides:
        count = lax.axis_size(axis)
        forward = [(i, i + 1) for i in range(count - 1)]
        backward = [(target, source) for source, target in forward]
        low = lax.ppermute(
            lax.slice_in_dim(block, block.shape[dim] - width, None, axis=dim), axis, forward
        )
        high = lax.ppermute(lax.slice_in_dim(block, 0, width, axis=dim), axis, backward)
        block = jnp.concatenate([low, block, high], axis=dim)
    return block


def face_weights(padded):
    wide = jnp.pad(padded, ((0, 0), (0, 0), (1, 1)))
    centre = wide[:, 1:-1, 1:-1]
    face_up = 0.5 * (centre + wide[:, 2:, 1:-1])
    face_down = 0.5 * (centre + wide[:, :-2, 1:-1])
    face_right = 0.5 * (centre + wide[:, 1:-1, 2:])
    face_left = 0.5 * (centre + wide[:, 1:-1, :-2])
    return (face_up + face_down + face_right + face_left, face_up, face_down, face_right, face_left)


def apply_faces(field, faces):
    middle = field[..., 1:-1, :]
    sideways = jnp.pad(middle, [(0, 0)] * (middle.ndim - 1) + [(1, 1)])
    total, face_up, face_down, face_right, face_left = faces
    return (
        total * middle
        - face_up * field[..., 2:, :]
        - face_down * field[..., :-2, :]
        - face_right * sideways[..., 2:]
        - face_left * sideways[..., :-2]
    )


def shards(rhs, coef, env):
    coef_padded = padded_2(coef, (("grid", 1),), 1)
    faces = tuple((weights[:, None] for weights in face_weights(coef_padded)))

    def square_sum(vector):
        return lax.psum(jnp.sum(vector * vector), ("grid", "rank"))

    solution = jnp.zeros(rhs.shape, jnp.float32)
    residual = rhs
    direction = rhs
    norm_now = square_sum(residual)
    for step in range(ITERS):
        padded = padded_2(direction, (("grid", 1),), 1)
        stenciled = apply_faces(padded[None], faces)
        image = lax.psum_scatter(
            jnp.einsum("krs,krxy->sxy", env, stenciled, precision=lax.Precision.HIGHEST),
            "rank",
            scatter_dimension=0,
            tiled=True,
        )
        image = lax.psum(image, "term")
        alpha = norm_now / lax.psum(jnp.sum(direction * image), ("grid", "rank"))
        solution = solution + alpha * direction
        residual = residual - alpha * image
        norm_next = square_sum(residual)
        direction = residual + norm_next / norm_now * direction
        norm_now = norm_next
    return (solution, residual)


def shift_sum(v):
    lane = lax.broadcasted_iota(jnp.int32, v.shape, v.ndim - 1)
    n = v.shape[-1]
    axis = v.ndim - 1
    left = jnp.where(lane == 0, 0.0, pltpu.roll(v, 1, axis))
    right = jnp.where(lane == n - 1, 0.0, pltpu.roll(v, n - 1, axis))
    return left + right


def neighbours(read, x, count):
    total = shift_sum(read(x))
    if x > 0:
        total = total + read(x - 1)
    if x < count - 1:
        total = total + read(x + 1)
    return total


def split3(v):
    high = v.astype(jnp.bfloat16)
    low = (v - high.astype(jnp.float32)).astype(jnp.bfloat16)
    return jnp.concatenate([high, high, low], axis=0)


def total_sum(v):
    return jnp.sum(v, axis=(0, 1), keepdims=True)


def cg_kernel(
    sizes,
    rhs_ref, coef_ref, env_ref,
    sol_ref, out_ref,
    env_all, coef_all, coef_tab, diag_tab, stack, residual, direction, image, partial, weighted, dots,
    rhs_send, rhs_recv, sib_send, sib_recv, env_send, env_recv, envy_send, envy_recv,
    coef_send, coef_recv, img_send, img_recv, dot_send, dot_recv,
):
    grids, ys, terms, per, rows, strip, ny, ranks = sizes
    nx = grids * strip
    half = ys * rows
    gx = lax.axis_index("grid")
    rank = lax.axis_index("rank")
    gz = lax.axis_index("term")
    gy = rank // 2
    core = rank % 2
    sibling = (gx, gy * 2 + (1 - core), gz)

    def at(dx, dy, dz):
        return ((gx + dx) % grids, ((gy + dy) % ys) * 2 + core, (gz + dz) % terms)

    peers = [at(dx, 0, dz) for dx in range(grids) for dz in range(terms) if dx or dz]
    peers += [at(dx, dy, 0) for dx in range(grids) for dy in range(1, ys)]
    peers.append(sibling)
    barrier = pltpu.get_barrier_semaphore()
    for peer in peers:
        pl.semaphore_signal(barrier, inc=1, device_id=peer, device_id_type=MESH)

    for i in range(strip):
        residual[gx * strip + i, gy, core] = rhs_ref[:, i, :]
    env_all[gz, :, gy] = env_ref[...]
    coef_all[gz, gx] = coef_ref[...]
    pl.semaphore_wait(barrier, len(peers))

    def remote(src, dst, send, recv, device):
        copy = pltpu.make_async_remote_copy(
            src_ref=src, dst_ref=dst, send_sem=send, recv_sem=recv, device_id=device, device_id_type=MESH
        )
        return copy

    def block_of(dx, dy, which):
        return residual.at[pl.ds(((gx + dx) % grids) * strip, strip), (gy + dy) % ys, which]

    own = block_of(0, 0, core)
    env_copies, envy_copies, rhs_copies, sib_copies, coef_copies = {}, {}, {}, {}, {}
    order = [1, terms - 1] + list(range(2, terms - 1))
    for dz in order:
        copy = remote(env_ref, env_all.at[gz, :, gy], env_send.at[dz], env_recv.at[dz], at(0, 0, dz))
        copy.start()
        env_copies[dz] = copy
    for dx in range(grids):
        for dy in range(ys):
            if dx or dy:
                d = dx * ys + dy
                copy = remote(own, own, rhs_send.at[d], rhs_recv.at[d], at(dx, dy, 0))
                copy.start()
                rhs_copies[d] = copy
    envy_copies[0] = remote(env_ref, env_all.at[gz, :, gy], envy_send.at[0], envy_recv.at[0], at(0, 1, 0))
    envy_copies[0].start()
    for dx in range(grids):
        for dz in range(terms):
            if dx or dz:
                d = dx * terms + dz
                copy = remote(coef_ref, coef_all.at[gz, gx], coef_send.at[d], coef_recv.at[d], at(dx, 0, dz))
                copy.start()
                coef_copies[d] = copy

    def to_sibling(dx, dy):
        d = dx * ys + dy
        block = block_of(dx, dy, core)
        copy = remote(block, block, sib_send.at[d], sib_recv.at[d], sibling)
        copy.start()
        sib_copies[d] = copy

    to_sibling(0, 0)
    for dx in range(grids):
        for dy in range(ys):
            if dx or dy:
                rhs_copies[dx * ys + dy].wait_recv()
                to_sibling(dx, dy)
    for dz in order:
        env_copies[dz].wait_recv()
        block = env_all.at[(gz - dz + terms) % terms, :, gy]
        copy = remote(block, block, envy_send.at[dz], envy_recv.at[dz], at(0, 1, 0))
        copy.start()
        envy_copies[dz] = copy

    for copy in coef_copies.values():
        copy.wait_recv()
    for x in range(nx):
        for z in range(terms):
            for i in range(per):
                k = z * per + i
                coef_tab[x, k : k + 1, :] = coef_all[z, x // strip, i, x % strip : x % strip + 1, :]
    for x in range(nx):
        diag_tab[x] = 0.5 * neighbours(lambda j: coef_tab[j], x, nx)

    for copy in sib_copies.values():
        copy.wait_recv()
    square = jnp.zeros((ranks, ny), jnp.float32)
    for x in range(nx):
        field = residual[x].reshape(ranks, ny)
        direction[x] = field
        square = square + field * field
    norm_now = total_sum(square)

    for copy in envy_copies.values():
        copy.wait_recv()
    for z in range(terms):
        for i in range(per):
            k = z * per + i
            block = env_all[z, i].reshape(half, ranks)
            high = block.astype(jnp.bfloat16)
            low = (block - high.astype(jnp.float32)).astype(jnp.bfloat16)
            stack[pl.ds(k * half, half), 0:ranks] = high
            stack[pl.ds(k * half, half), ranks : 2 * ranks] = low
            stack[pl.ds(k * half, half), 2 * ranks : 3 * ranks] = high
    for copies in (env_copies, envy_copies, rhs_copies, sib_copies, coef_copies):
        for copy in copies.values():
            copy.wait_send()

    count = terms * per

    def product(x):
        field = direction[x]
        wide = 2.0 * field - 0.5 * neighbours(lambda j: direction[j], x, nx)
        plain = jnp.dot(stack[...], split3(field), preferred_element_type=jnp.float32)
        spread = jnp.dot(stack[...], split3(wide), preferred_element_type=jnp.float32)
        total = jnp.zeros((half, ny), jnp.float32)
        inner = jnp.zeros((half, ny), jnp.float32)
        for k in range(count):
            c = coef_tab[x, k : k + 1, :]
            d = diag_tab[x, k : k + 1, :]
            u = plain[k * half : (k + 1) * half]
            total = total + c * spread[k * half : (k + 1) * half] + d * u
            inner = inner + c * u
        partial[x] = total
        weighted[x] = inner

    def finish(x, slot):
        value = partial[x] - 0.5 * neighbours(lambda j: weighted[j], x, nx)
        image[slot, x, :, core] = value.reshape(ys, rows, ny)

    def image_copy(x, slot):
        block = image.at[slot, x, :, core]
        return remote(block, block, img_send.at[slot, x], img_recv.at[slot, x], sibling)

    def operate(slot, send):
        for x in range(nx + 1):
            if x < nx:
                product(x)
            if x > 0:
                finish(x - 1, slot)
                if send:
                    image_copy(x - 1, slot).start()

    strips = pl.ds(gx * strip, strip)

    def iteration(step, norm_now):
        slot = step % 2
        operate(slot, True)
        product_sum = jnp.zeros((ranks, ny), jnp.float32)
        for x in range(nx):
            image_copy(x, slot).wait_recv()
            product_sum = product_sum + direction[x] * image[slot, x].reshape(ranks, ny)
        alpha = norm_now / total_sum(product_sum)
        square = jnp.zeros((ranks, ny), jnp.float32)
        for x in range(nx):
            fresh = residual[x].reshape(ranks, ny) - alpha * image[slot, x].reshape(ranks, ny)
            residual[x] = fresh.reshape(ys, 2, rows, ny)
            square = square + fresh * fresh
        norm_next = total_sum(square)
        beta = norm_next / norm_now
        mine = pl.ds(pl.multiple_of(rank * rows, rows), rows)
        for i in range(strip):
            sol_ref[i] = sol_ref[i] + alpha * direction[gx * strip + i, mine, :]
        for x in range(nx):
            direction[x] = residual[x].reshape(ranks, ny) + beta * direction[x]
        for x in range(nx):
            image_copy(x, slot).wait_send()
        return norm_next

    sol_ref[...] = jnp.zeros_like(sol_ref)
    norm_now = lax.fori_loop(0, ITERS - 1, iteration, norm_now)

    slot = (ITERS - 1) % 2
    operate(slot, False)
    mine = pl.ds(pl.multiple_of(rank * rows, rows), rows)
    part = jnp.zeros((rows, ny), jnp.float32)
    for x in range(nx):
        for y in range(ys):
            field = direction[x, pl.ds(pl.multiple_of((y * 2 + core) * rows, rows), rows), :]
            part = part + field * image[slot, x, y, core]
    dots[core] = jnp.broadcast_to(total_sum(part), (8, 128))
    copy = remote(dots.at[core], dots.at[core], dot_send, dot_recv, sibling)
    copy.start()
    copy.wait()
    both = dots[0] + dots[1]
    alpha = norm_now / both[0:1, 0:1]
    for i in range(strip):
        x = gx * strip + i
        sol_ref[i] = sol_ref[i] + alpha * direction[x, mine, :]
        out_ref[i] = residual[x, gy, core] - alpha * image[slot, x, gy, core]


def fused(mesh, rhs, coef, env):
    grids, rank_shards, terms = (mesh.shape[a] for a in ("grid", "rank", "term"))
    ys = rank_shards // 2
    rows, strip, ny = rhs.shape
    per, ranks = env.shape[0], env.shape[2]
    nx, half, count = grids * strip, ys * rows, per * terms
    sizes = (grids, ys, terms, per, rows, strip, ny, ranks)
    f32 = jnp.float32
    dma = pltpu.SemaphoreType.DMA
    block = jax.ShapeDtypeStruct((strip, rows, ny), f32)
    sol, res = pl.pallas_call(
        functools.partial(cg_kernel, sizes),
        out_shape=(block, block),
        in_specs=[pl.BlockSpec(memory_space=pltpu.VMEM)] * 3,
        out_specs=(pl.BlockSpec(memory_space=pltpu.VMEM),) * 2,
        scratch_shapes=[
            pltpu.VMEM((terms, per, ys, rows, ranks), f32),
            pltpu.VMEM((terms, grids, per, strip, ny), f32),
            pltpu.VMEM((nx, count, ny), f32),
            pltpu.VMEM((nx, count, ny), f32),
            pltpu.VMEM((count * half, 3 * ranks), jnp.bfloat16),
            pltpu.VMEM((nx, ys, 2, rows, ny), f32),
            pltpu.VMEM((nx, ranks, ny), f32),
            pltpu.VMEM((2, nx, ys, 2, rows, ny), f32),
            pltpu.VMEM((nx, half, ny), f32),
            pltpu.VMEM((nx, half, ny), f32),
            pltpu.VMEM((2, 8, 128), f32),
            dma((grids * ys,)), dma((grids * ys,)),
            dma((grids * ys,)), dma((grids * ys,)),
            dma((terms,)), dma((terms,)),
            dma((terms,)), dma((terms,)),
            dma((grids * terms,)), dma((grids * terms,)),
            dma((2, nx)), dma((2, nx)),
            dma, dma,
        ],
        compiler_params=pltpu.CompilerParams(
            collective_id=0, has_side_effects=True, vmem_limit_bytes=48 * 2**20
        ),
    )(rhs, coef, env)
    return sol.transpose(1, 0, 2), res.transpose(1, 0, 2)


def fits(mesh, rhs):
    cells = rhs.shape[1] * mesh.shape["grid"] * rhs.shape[2]
    return mesh.shape["rank"] == 4 and rhs.shape[0] * 4 * cells * 4 <= 2**20


def solution(mesh):
    placed = (P("rank", "grid", None), P("term", "grid", None), P("term", "rank", None))

    def run(rhs, coef, env):
        if fits(mesh, rhs):
            return fused(mesh, rhs, coef, env)
        return shards(rhs, coef, env)

    return jax.shard_map(
        run,
        mesh=mesh,
        in_specs=placed,
        out_specs=(P("rank", "grid", None), P("rank", "grid", None)),
        check_vma=False,
    )
```

```python
import functools

import jax
import jax.numpy as jnp
from jax import lax
from jax.experimental import pallas as pl
from jax.experimental.pallas import tpu as pltpu
from jax.sharding import PartitionSpec as P

ITERS = 4
MESH = pl.DeviceIdType.MESH


def padded_2(block, sides, width):
    for axis, dim in sides:
        count = lax.axis_size(axis)
        forward = [(i, i + 1) for i in range(count - 1)]
        backward = [(target, source) for source, target in forward]
        low = lax.ppermute(
            lax.slice_in_dim(block, block.shape[dim] - width, None, axis=dim), axis, forward
        )
        high = lax.ppermute(lax.slice_in_dim(block, 0, width, axis=dim), axis, backward)
        block = jnp.concatenate([low, block, high], axis=dim)
    return block


def face_weights(padded):
    wide = jnp.pad(padded, ((0, 0), (0, 0), (1, 1)))
    centre = wide[:, 1:-1, 1:-1]
    face_up = 0.5 * (centre + wide[:, 2:, 1:-1])
    face_down = 0.5 * (centre + wide[:, :-2, 1:-1])
    face_right = 0.5 * (centre + wide[:, 1:-1, 2:])
    face_left = 0.5 * (centre + wide[:, 1:-1, :-2])
    return (face_up + face_down + face_right + face_left, face_up, face_down, face_right, face_left)


def apply_faces(field, faces):
    middle = field[..., 1:-1, :]
    sideways = jnp.pad(middle, [(0, 0)] * (middle.ndim - 1) + [(1, 1)])
    total, face_up, face_down, face_right, face_left = faces
    return (
        total * middle
        - face_up * field[..., 2:, :]
        - face_down * field[..., :-2, :]
        - face_right * sideways[..., 2:]
        - face_left * sideways[..., :-2]
    )


def shards(rhs, coef, env):
    coef_padded = padded_2(coef, (("grid", 1),), 1)
    faces = tuple((weights[:, None] for weights in face_weights(coef_padded)))

    def square_sum(vector):
        return lax.psum(jnp.sum(vector * vector), ("grid", "rank"))

    solution = jnp.zeros(rhs.shape, jnp.float32)
    residual = rhs
    direction = rhs
    norm_now = square_sum(residual)
    for step in range(ITERS):
        padded = padded_2(direction, (("grid", 1),), 1)
        stenciled = apply_faces(padded[None], faces)
        image = lax.psum_scatter(
            jnp.einsum("krs,krxy->sxy", env, stenciled, precision=lax.Precision.HIGHEST),
            "rank",
            scatter_dimension=0,
            tiled=True,
        )
        image = lax.psum(image, "term")
        alpha = norm_now / lax.psum(jnp.sum(direction * image), ("grid", "rank"))
        solution = solution + alpha * direction
        residual = residual - alpha * image
        norm_next = square_sum(residual)
        direction = residual + norm_next / norm_now * direction
        norm_now = norm_next
    return (solution, residual)


def shift_sum(v):
    lane = lax.broadcasted_iota(jnp.int32, v.shape, v.ndim - 1)
    n = v.shape[-1]
    axis = v.ndim - 1
    left = jnp.where(lane == 0, 0.0, pltpu.roll(v, 1, axis))
    right = jnp.where(lane == n - 1, 0.0, pltpu.roll(v, n - 1, axis))
    return left + right


def neighbours(read, x, count):
    total = shift_sum(read(x))
    if x > 0:
        total = total + read(x - 1)
    if x < count - 1:
        total = total + read(x + 1)
    return total


def split3(v):
    high = v.astype(jnp.bfloat16)
    low = (v - high.astype(jnp.float32)).astype(jnp.bfloat16)
    return jnp.concatenate([high, high, low], axis=0)


def total_sum(v):
    return jnp.sum(v, axis=(0, 1), keepdims=True)


def cg_kernel(
    sizes,
    rhs_ref, coef_ref, env_ref,
    sol_ref, out_ref,
    rhs_own, env_all, coef_all, coef_tab, diag_tab, stack, residual, direction, image, partial, weighted, dots,
    load, rhs_send, rhs_recv, sib_send, sib_recv, env_send, env_recv, envy_send, envy_recv,
    coef_send, coef_recv, img_send, img_recv, dot_send, dot_recv,
):
    terms, per, rows, strip, ny, ranks = sizes
    grids, ys = 2, 2
    nx = grids * strip
    half = ys * rows
    gx = lax.axis_index("grid")
    rank = lax.axis_index("rank")
    gz = lax.axis_index("term")
    gy = rank // 2
    core = rank % 2
    sibling = (gx, gy * 2 + (1 - core), gz)

    def at(x, y, z):
        return (x, y * 2 + core, z)

    origins = [gz + 1 - 2 * (gz % 2), 2 - gz // 2, 3 - 3 * (gz // 2)]
    over_x, over_y, across = at(1 - gx, gy, gz), at(gx, 1 - gy, gz), at(1 - gx, 1 - gy, gz)
    line = [at(gx, gy, o) for o in origins]

    loads = [
        pltpu.make_async_copy(rhs_ref, rhs_own, load.at[0]),
        pltpu.make_async_copy(env_ref, env_all.at[gz, :, gy], load.at[1]),
        pltpu.make_async_copy(coef_ref, coef_all.at[gz, gx], load.at[2]),
    ]
    for copy in loads:
        copy.start()

    barrier = pltpu.get_barrier_semaphore()

    def greet(peer):
        pl.semaphore_signal(barrier, inc=1, device_id=peer, device_id_type=MESH)

    peers = line + [over_x, over_y, across, sibling]
    for peer in peers:
        greet(peer)

    loads[0].wait()
    for i in range(strip):
        residual[gx * strip + i, gy, core] = rhs_own[:, i, :]
    loads[1].wait()
    loads[2].wait()
    pl.semaphore_wait(barrier, len(peers))

    sent = []

    def remote(src, dst, send, recv, device):
        return pltpu.make_async_remote_copy(
            src_ref=src, dst_ref=dst, send_sem=send, recv_sem=recv, device_id=device, device_id_type=MESH
        )

    def push(block, send, recv, device):
        copy = remote(block, block, send, recv, device)
        sent.append(copy)
        copy.start()
        return copy

    def arrived(block, recv):
        remote(block, block, dot_send, recv, sibling).wait_recv()

    def strip_of(x, y):
        return residual.at[pl.ds(x * strip, strip), y, core]

    def env_line(o):
        return env_all.at[o, :, gy]

    own = strip_of(gx, gy)
    for i in (2, 1, 0):
        push(env_line(gz), env_send.at[i], env_recv.at[gz], line[i])
    rhs_y = push(own, rhs_send.at[0], rhs_recv.at[0], over_y)
    rhs_x = push(own, rhs_send.at[1], rhs_recv.at[1], over_x)
    rhs_d = push(own, rhs_send.at[2], rhs_recv.at[2], across)
    for i in (2, 1, 0):
        push(coef_all.at[gz, gx], coef_send.at[i], coef_recv.at[gz], line[i])
    push(env_line(gz), envy_send.at[3], envy_recv.at[gz], over_y)
    sibs = [push(own, sib_send.at[0], sib_recv.at[0], sibling)]

    def put_stack(o):
        for i in range(per):
            block = env_all[o, i].reshape(half, ranks)
            high = block.astype(jnp.bfloat16)
            low = (block - high.astype(jnp.float32)).astype(jnp.bfloat16)
            at = pl.ds(pl.multiple_of((o * per + i) * half, half), half)
            stack[at, 0:ranks] = high
            stack[at, ranks : 2 * ranks] = low
            stack[at, 2 * ranks : 3 * ranks] = high

    def cross(i):
        o = origins[i]
        arrived(env_line(o), env_recv.at[o])
        push(env_line(o), envy_send.at[i], envy_recv.at[o], over_y)

    def to_sibling(i, copy, x, y):
        copy.wait_recv()
        sibs.append(push(strip_of(x, y), sib_send.at[i], sib_recv.at[i], sibling))

    def crossed_into_stack(o):
        arrived(env_all.at[o, :, 1 - gy], envy_recv.at[o])
        put_stack(o)

    cross(0)
    to_sibling(1, rhs_y, gx, 1 - gy)
    to_sibling(2, rhs_x, 1 - gx, gy)
    to_sibling(3, rhs_d, 1 - gx, 1 - gy)
    cross(1)
    for o in origins:
        arrived(coef_all.at[o, gx], coef_recv.at[o])
    coef_x = push(coef_all.at[:, gx], coef_send.at[terms - 1], coef_recv.at[gz], over_x)
    cross(2)
    coef_x.wait_recv()
    for x in range(nx):
        for z in range(terms):
            for i in range(per):
                k = z * per + i
                coef_tab[x, k : k + 1, :] = coef_all[z, x // strip, i, x % strip : x % strip + 1, :]
    for x in range(nx):
        diag_tab[x] = 0.5 * neighbours(lambda j: coef_tab[j], x, nx)
    for copy in sibs:
        copy.wait_recv()
    square = jnp.zeros((ranks, ny), jnp.float32)
    for x in range(nx):
        field = residual[x].reshape(ranks, ny)
        direction[x] = field
        square = square + field * field
    norm_now = total_sum(square)
    for o in [gz] + origins:
        crossed_into_stack(o)
    for copy in sent:
        copy.wait_send()

    count = terms * per

    def product(x):
        field = direction[x]
        wide = 2.0 * field - 0.5 * neighbours(lambda j: direction[j], x, nx)
        plain = jnp.dot(stack[...], split3(field), preferred_element_type=jnp.float32)
        spread = jnp.dot(stack[...], split3(wide), preferred_element_type=jnp.float32)
        total = jnp.zeros((half, ny), jnp.float32)
        inner = jnp.zeros((half, ny), jnp.float32)
        for k in range(count):
            c = coef_tab[x, k : k + 1, :]
            d = diag_tab[x, k : k + 1, :]
            u = plain[k * half : (k + 1) * half]
            total = total + c * spread[k * half : (k + 1) * half] + d * u
            inner = inner + c * u
        partial[x] = total
        weighted[x] = inner

    def finish(x, slot):
        value = partial[x] - 0.5 * neighbours(lambda j: weighted[j], x, nx)
        image[slot, x, :, core] = value.reshape(ys, rows, ny)

    def image_copy(x, slot):
        block = image.at[slot, x, :, core]
        return remote(block, block, img_send.at[slot, x], img_recv.at[slot, x], sibling)

    def operate(slot, send):
        for x in range(nx + 1):
            if x < nx:
                product(x)
            if x > 0:
                finish(x - 1, slot)
                if send:
                    image_copy(x - 1, slot).start()

    strips = pl.ds(gx * strip, strip)

    def iteration(step, norm_now):
        slot = step % 2
        operate(slot, True)
        product_sum = jnp.zeros((ranks, ny), jnp.float32)
        for x in range(nx):
            image_copy(x, slot).wait_recv()
            product_sum = product_sum + direction[x] * image[slot, x].reshape(ranks, ny)
        alpha = norm_now / total_sum(product_sum)
        square = jnp.zeros((ranks, ny), jnp.float32)
        for x in range(nx):
            fresh = residual[x].reshape(ranks, ny) - alpha * image[slot, x].reshape(ranks, ny)
            residual[x] = fresh.reshape(ys, 2, rows, ny)
            square = square + fresh * fresh
        norm_next = total_sum(square)
        beta = norm_next / norm_now
        mine = pl.ds(pl.multiple_of(rank * rows, rows), rows)
        for i in range(strip):
            sol_ref[i] = sol_ref[i] + alpha * direction[gx * strip + i, mine, :]
        for x in range(nx):
            direction[x] = residual[x].reshape(ranks, ny) + beta * direction[x]
        for x in range(nx):
            image_copy(x, slot).wait_send()
        return norm_next

    sol_ref[...] = jnp.zeros_like(sol_ref)
    norm_now = lax.fori_loop(0, ITERS - 1, iteration, norm_now)

    slot = (ITERS - 1) % 2
    operate(slot, False)
    mine = pl.ds(pl.multiple_of(rank * rows, rows), rows)
    part = jnp.zeros((rows, ny), jnp.float32)
    for x in range(nx):
        for y in range(ys):
            field = direction[x, pl.ds(pl.multiple_of((y * 2 + core) * rows, rows), rows), :]
            part = part + field * image[slot, x, y, core]
    dots[core] = jnp.broadcast_to(total_sum(part), (8, 128))
    copy = remote(dots.at[core], dots.at[core], dot_send, dot_recv, sibling)
    copy.start()
    copy.wait()
    both = dots[0] + dots[1]
    alpha = norm_now / both[0:1, 0:1]
    for i in range(strip):
        x = gx * strip + i
        sol_ref[i] = sol_ref[i] + alpha * direction[x, mine, :]
        out_ref[i] = residual[x, gy, core] - alpha * image[slot, x, gy, core]


def fused(mesh, rhs, coef, env):
    terms = mesh.shape["term"]
    rows, strip, ny = rhs.shape
    per, ranks = env.shape[0], env.shape[2]
    grids, ys = 2, 2
    nx, half, count = grids * strip, ys * rows, per * terms
    sizes = (terms, per, rows, strip, ny, ranks)
    f32 = jnp.float32
    dma = pltpu.SemaphoreType.DMA
    block = jax.ShapeDtypeStruct((strip, rows, ny), f32)
    sol, res = pl.pallas_call(
        functools.partial(cg_kernel, sizes),
        out_shape=(block, block),
        in_specs=[pl.BlockSpec(memory_space=pltpu.HBM)] * 3,
        out_specs=(pl.BlockSpec(memory_space=pltpu.VMEM),) * 2,
        scratch_shapes=[
            pltpu.VMEM((rows, strip, ny), f32),
            pltpu.VMEM((terms, per, ys, rows, ranks), f32),
            pltpu.VMEM((terms, grids, per, strip, ny), f32),
            pltpu.VMEM((nx, count, ny), f32),
            pltpu.VMEM((nx, count, ny), f32),
            pltpu.VMEM((count * half, 3 * ranks), jnp.bfloat16),
            pltpu.VMEM((nx, ys, 2, rows, ny), f32),
            pltpu.VMEM((nx, ranks, ny), f32),
            pltpu.VMEM((2, nx, ys, 2, rows, ny), f32),
            pltpu.VMEM((nx, half, ny), f32),
            pltpu.VMEM((nx, half, ny), f32),
            pltpu.VMEM((2, 8, 128), f32),
            dma((3,)),
            dma((3,)), dma((3,)),
            dma((4,)), dma((4,)),
            dma((terms - 1,)), dma((terms,)),
            dma((terms,)), dma((terms,)),
            dma((terms,)), dma((terms,)),
            dma((2, nx)), dma((2, nx)),
            dma, dma,
        ],
        compiler_params=pltpu.CompilerParams(
            collective_id=0, has_side_effects=True, vmem_limit_bytes=63 * 2**20
        ),
    )(rhs, coef, env)
    return sol.transpose(1, 0, 2), res.transpose(1, 0, 2)


def fits(mesh, rhs):
    cells = rhs.shape[1] * mesh.shape["grid"] * rhs.shape[2]
    return mesh.shape["rank"] == 4 and mesh.shape["grid"] == 2 and mesh.shape["term"] == 4 and rhs.shape[0] * 4 * cells * 4 <= 2**20


def solution(mesh):
    placed = (P("rank", "grid", None), P("term", "grid", None), P("term", "rank", None))

    def run(rhs, coef, env):
        if fits(mesh, rhs):
            return fused(mesh, rhs, coef, env)
        return shards(rhs, coef, env)

    return jax.shard_map(
        run,
        mesh=mesh,
        in_specs=placed,
        out_specs=(P("rank", "grid", None), P("rank", "grid", None)),
        check_vma=False,
    )
```
